512 devices in a mesh: section: 16 (over x, y_lo, core), fsdp: 32 (over z, y_hi).
Axes of the slice: x: 4, y: 4 (y_hi: 2, y_lo: 2; y = y_hi * 2 + y_lo), z: 16, core: 2. Of those that a mesh axis runs over, the one named last changes fastest.
Arguments:
- acts: bfloat16 [16, 2, 512, 16384], P('section', None, None, 'fsdp'), may hold values from -6 to 6
- gate_up_weight: bfloat16 [16, 16384, 2048], P('section', 'fsdp'), may hold values from -0.046875 to 0.046875
- down_weight: bfloat16 [16, 1024, 16384], P('section', None, 'fsdp'), may hold values from -0.1875 to 0.1875
Outputs:
- arrived: bfloat16 [16, 2, 512, 16384], P('section', None, None, 'fsdp')
The draws below stay inside these ranges and needn't reach their ends.
All inputs are finite; a program needn't handle non-finite values.
Results may differ from the reference program's by a relative error of at most 0.0037.
Values may be sent and summed in bfloat16 or wider, within the bound.
No kernel may reach another device: no remote copies, remote signals or barrier semaphores. Data moves between devices by JAX's collectives and lax.ppermute only.
A program may use at most 64 MiB of HBM per device.

```python
import jax
import jax.numpy as jnp
from jax import lax

D = 16384
F = 1024
MB_TOK = 512
MICRO = 2
SECTIONS = 16


def block_levels(own_key, dims, shards, smallest, top_value):
    level = 1.0
    for position, parts in shards:
        steps = jax.random.uniform(jax.random.fold_in(jax.random.fold_in(own_key, 6), position), (parts,), jnp.float32, smallest / len(shards), top_value / len(shards))
        level = level * jnp.repeat(jnp.exp(steps), dims[position] // parts).reshape((-1,) + (1,) * (len(dims) - 1 - position))
    return level


def gaussian(stream_key, dims, width, reach, pieces=(), held_as=jnp.bfloat16):
    array = jax.random.normal(stream_key, dims, jnp.float32) * width
    if len(pieces) > 0:
        array = block_levels(stream_key, dims, pieces, -0.22, 0.18) * array
    return jnp.clip(array, min=-reach, max=reach).astype(held_as)


def setup_inputs(seed: int = 0) -> dict:
    key_list = jax.random.split(jax.random.key(seed), 4)
    return {
        "acts": gaussian(key_list[0], (SECTIONS, MICRO, MB_TOK, D), 1.0, 6.0, ((0, 16), (3, 32))),
        "gate_up_weight": gaussian(key_list[1], (SECTIONS, D, 2 * F), D ** -0.5, 0.046875, ((0, 16), (1, 32))),
        "down_weight": gaussian(key_list[2], (SECTIONS, F, D), F ** -0.5, 0.1875, ((0, 16), (2, 32))),
    }


def reference(acts, gate_up_weight, down_weight):
    def one_section(operands):
        section_acts, weight_in, weight_out = operands

        def one_batch(rows):
            summed = jnp.dot(rows, weight_in, preferred_element_type=jnp.float32)
            hidden = (jax.nn.silu(summed[:, :F]) * summed[:, F:]).astype(jnp.bfloat16)
            branch = jnp.dot(hidden, weight_out, preferred_element_type=jnp.float32)
            return (rows.astype(jnp.float32) + branch).astype(jnp.bfloat16)

        return lax.map(one_batch, section_acts)

    updated = lax.map(one_section, (acts, gate_up_weight, down_weight))
    return jnp.roll(updated, 1, axis=0)
```

```python
import jax
import jax.numpy as jnp
from jax import lax
from jax.sharding import Mesh, PartitionSpec as P

SECTIONS, RING, PAIR = 16, 16, 2


def to_next_section(block):
    return lax.ppermute(block, "section", [(i, (i + 1) % SECTIONS) for i in range(SECTIONS)])


def to_next_section_pair(block, flip):
    route = [
        (s * PAIR + y, (s + 1) % SECTIONS * PAIR + (y ^ flip))
        for s in range(SECTIONS)
        for y in range(PAIR)
    ]
    return lax.ppermute(block, ("section", "pair"), route)


def body(acts, gate_up_weight, down_weight):
    rows = acts.shape[1] * acts.shape[2]
    inputs = acts[0].reshape(rows, acts.shape[3])
    terms = jnp.dot(inputs, gate_up_weight[0], preferred_element_type=jnp.float32)
    inputs = to_next_section(inputs)
    weight_out = to_next_section(down_weight[0])
    summed = lax.psum_scatter(terms, "ring", scatter_dimension=0, tiled=True)
    summed = summed.astype(jnp.bfloat16)
    same = to_next_section_pair(summed, 0)
    other = to_next_section_pair(summed, 1)
    projected = same.astype(jnp.float32) + other.astype(jnp.float32)
    width = weight_out.shape[0]
    hidden = (jax.nn.silu(projected[:, :width]) * projected[:, width:]).astype(jnp.bfloat16)
    hidden = lax.all_gather(hidden, "ring", axis=0, tiled=True)
    branch = jnp.dot(hidden, weight_out, preferred_element_type=jnp.float32)
    updated = (inputs.astype(jnp.float32) + branch).astype(jnp.bfloat16)
    return updated.reshape(acts.shape)


def solution(mesh):
    split = Mesh(mesh.devices.reshape(SECTIONS, RING, PAIR), ("section", "ring", "pair"))
    fsdp = ("ring", "pair")
    return jax.shard_map(
        body,
        mesh=split,
        in_specs=(
            P("section", None, None, fsdp),
            P("section", fsdp, None),
            P("section", None, fsdp),
        ),
        out_specs=P("section", None, None, fsdp),
        check_vma=False,
    )
```

```python
import jax
import jax.numpy as jnp
from jax import lax
from jax.sharding import Mesh, PartitionSpec as P

SECTIONS, OUTER, INNER, PAIR = 16, 4, 4, 2
BF16, F32 = jnp.bfloat16, jnp.float32


def swap_pair(block):
    return lax.ppermute(block, "pair", [(0, 1), (1, 0)])


def next_section(block, flip):
    route = [
        (s * PAIR + y, (s + 1) % SECTIONS * PAIR + (y ^ flip))
        for s in range(SECTIONS)
        for y in range(PAIR)
    ]
    return lax.ppermute(block, ("section", "pair"), route)


def inner_shift(block, distance):
    return lax.ppermute(block, "inner", [(i, (i + distance) % INNER) for i in range(INNER)])


def pick(array, index, axis):
    return lax.dynamic_index_in_dim(array, index, axis, keepdims=False)


def swiglu(projected, width):
    return (jax.nn.silu(projected[:, :width]) * projected[:, width:]).astype(BF16)


def exchange_sum(terms, axis, parts):
    got = lax.all_to_all(terms, axis, split_axis=0, concat_axis=0, tiled=True)
    got = got.reshape(parts, terms.shape[0] // parts, terms.shape[1]).astype(F32)
    return jnp.sum(got, axis=0)


def body(acts, gate_up_weight, down_weight):
    weight_in, weight_out = gate_up_weight[0], down_weight[0]
    width, columns = weight_out.shape
    batches, tokens = acts.shape[1:3]
    me, inner = lax.axis_index("pair"), lax.axis_index("inner")
    share = tokens // (PAIR * INNER * OUTER)
    halves = acts[0].reshape(batches, PAIR, tokens // PAIR, columns)

    sent = jnp.dot(pick(halves[1], 1 - me, 0), weight_in, preferred_element_type=F32).astype(BF16)
    swapped = swap_pair(sent)

    ring_rows = acts[0, 0].reshape(PAIR, INNER, OUTER, share, columns).transpose(2, 1, 0, 3, 4)
    ring_terms = jnp.dot(ring_rows.reshape(tokens, columns), weight_in, preferred_element_type=F32)
    ring_sum = lax.psum_scatter(ring_terms, ("outer", "inner"), scatter_dimension=0, tiled=True)

    kept = jnp.dot(pick(halves[1], me, 0), weight_in, preferred_element_type=F32)
    paired = (kept + swapped.astype(F32)).astype(BF16)
    run_sum = exchange_sum(paired, "inner", INNER).astype(BF16)

    mine, other = pick(halves, me, 1), pick(halves, 1 - me, 1)
    (mine, other, weight_out), run_sum = lax.optimization_barrier(((mine, other, weight_out), run_sum))
    residual_mine, residual_other = next_section(mine, 0), next_section(other, 1)
    weight_mine, weight_other = next_section(weight_out, 0), next_section(weight_out, 1)

    swap_hidden = swiglu(exchange_sum(run_sum, "outer", OUTER), width)
    swap_hidden = next_section(swap_hidden, 0)

    ring_half = ring_sum.astype(BF16).reshape(PAIR, share, 2 * width)
    ring_mine = next_section(pick(ring_half, me, 0), 0)
    ring_other = next_section(pick(ring_half, 1 - me, 0), 1)
    ring_hidden = swiglu(ring_mine.astype(F32) + ring_other.astype(F32), width)

    hidden = jnp.concatenate([ring_hidden, swap_hidden])
    hidden = lax.all_gather(hidden, "outer", axis=0, tiled=True)
    hidden = hidden.reshape(OUTER, batches, share, width).transpose(1, 0, 2, 3)
    hidden = hidden.reshape(batches * OUTER * share, width)

    weight_both = jnp.concatenate([weight_mine, weight_other], axis=1)
    residual_both = jnp.concatenate([residual_mine, residual_other], axis=2)
    residual_both = residual_both.reshape(batches, INNER, OUTER * share, 2 * columns)
    out = jnp.zeros((batches, PAIR, INNER, OUTER * share, columns), BF16)
    distances = ((0, 1), (3, 2))
    pieces = {d: inner_shift(hidden, d) if d else hidden for d in (0, 1, 3, 2)}
    for group in distances:
        updates = []
        for d in group:
            place = (inner - d) % INNER
            branch = jnp.dot(pieces[d], weight_both, preferred_element_type=F32)
            residual = pick(residual_both, place, 1).reshape(branch.shape)
            updates.append((residual.astype(F32) + branch).astype(BF16))
        foreign = swap_pair(jnp.stack([u[:, columns:] for u in updates]))
        for n, d in enumerate(group):
            place = (inner - d) % INNER
            shape = (batches, 1, 1, OUTER * share, columns)
            out = lax.dynamic_update_slice(out, updates[n][:, :columns].reshape(shape), (0, me, place, 0, 0))
            out = lax.dynamic_update_slice(out, foreign[n].reshape(shape), (0, 1 - me, place, 0, 0))
    return out.reshape(acts.shape)


def solution(mesh):
    split = Mesh(
        mesh.devices.reshape(SECTIONS, OUTER, INNER, PAIR), ("section", "outer", "inner", "pair")
    )
    fsdp = ("outer", "inner", "pair")
    return jax.shard_map(
        body,
        mesh=split,
        in_specs=(
            P("section", None, None, fsdp),
            P("section", fsdp, None),
            P("section", None, fsdp),
        ),
        out_specs=P("section", None, None, fsdp),
        check_vma=False,
    )
```
